32 devices in a mesh: seq: 16 (over z, y, x), head: 2 (over core).
Axes of the slice: x: 2, y: 2, z: 4, core: 2. Of those that a mesh axis runs over, the one named last changes fastest.
Arguments:
- q_delta: bfloat16 [4096, 2048], P('seq', 'head'), may hold values from -6 to 6
- k_delta: bfloat16 [4096, 2048], P('seq', 'head'), may hold values from -6 to 6
- v_delta: bfloat16 [4096, 2048], P('seq', 'head'), may hold values from -6 to 6
- write_rate: float32 [4096, 16], P('seq', 'head'), may hold values from 0 to 1
- q_attn: bfloat16 [4096, 2048], P('seq', 'head'), may hold values from -200 to 200
- k_attn: bfloat16 [4096, 2048], P('seq', 'head'), may hold values from -6 to 6
- out_gain: float32 [2048], P('head'), may hold values from 0.5 to 1.5
Outputs:
- delta_out: bfloat16 [4096, 2048], P('seq', 'head')
- normed_out: bfloat16 [4096, 2048], P('seq', 'head')
The draws below stay inside these ranges and needn't reach their ends.
All inputs are finite; a program needn't handle non-finite values.
Results may differ from the reference program's by a relative error of at most 0.0058.
Values may be sent and summed in bfloat16 or wider, within the bound.
A program may use at most 64 MiB of HBM per device.

```python
import math
import jax
import jax.numpy as jnp
from jax import lax

HEAD_COUNT = 16
HD = 128
GROUP_TOKENS = 64
WINDOW = 2048
TOK_DEV = 256
SEQUENCE_TOKENS = 4096
D = 2048


def draw_write_rate(key, part):
    rate_random_key, noise_random_key, block_random_key, spike_random_key = jax.random.split(jax.random.fold_in(key, 3), 4)
    slowest = 64.0 / SEQUENCE_TOKENS
    mixture = jax.random.uniform(rate_random_key, (HEAD_COUNT,))
    head_rate = jnp.exp(jnp.log(slowest) * (1.0 - mixture))
    jitter = jax.random.uniform(noise_random_key, (SEQUENCE_TOKENS, HEAD_COUNT), minval=0.5, maxval=1.5)
    block_scale = jnp.exp(jax.random.uniform(block_random_key, (SEQUENCE_TOKENS // TOK_DEV, HEAD_COUNT), minval=-0.7, maxval=0.7))
    block_scale = jnp.repeat(block_scale, TOK_DEV, axis=0)
    sampled_rate = jnp.minimum(head_rate[None, :] * jitter * block_scale, 1.0)
    spike_positions = jax.random.randint(spike_random_key, (4, HEAD_COUNT), 0, SEQUENCE_TOKENS // GROUP_TOKENS)
    group_lookup = jnp.arange(SEQUENCE_TOKENS) // GROUP_TOKENS
    inside_spike = jnp.any(group_lookup[:, None, None] == spike_positions[None, :, :], axis=1)
    return jnp.where(inside_spike, 0.9, sampled_rate).astype(jnp.float32)


def attention_pair(key):
    query_key, keys_key = jax.random.split(jax.random.fold_in(key, 7), 2)
    queries = jax.random.truncated_normal(query_key, -6.0, 6.0, (SEQUENCE_TOKENS, D), jnp.float32)
    base_keys = jax.random.truncated_normal(keys_key, -6.0, 6.0, (SEQUENCE_TOKENS, D), jnp.float32)
    key_rows = base_keys
    return (queries, key_rows)


def draw_q_attn(key, part):
    return attention_pair(key)[0].astype(jnp.bfloat16)


def draw_k_attn(key, part):
    return attention_pair(key)[1].astype(jnp.bfloat16)


def level_of(key, dims, pieces, low, high):
    factor_of = 1.0
    for dim, shards_of in pieces:
        heights = jax.random.uniform(jax.random.fold_in(jax.random.fold_in(key, 6), dim), (shards_of,), jnp.float32, low / len(pieces), high / len(pieces))
        factor_of = factor_of * jnp.repeat(jnp.exp(heights), dims[dim] // shards_of).reshape((-1,) + (1,) * (len(dims) - 1 - dim))
    return factor_of


def bell_draw(rng, shape, width, most, cuts=(), held_as=jnp.bfloat16):
    values = jax.random.normal(rng, shape, jnp.float32) * width
    if len(cuts) > 0:
        values = level_of(rng, shape, cuts, -0.22, 0.18) * values
    return jnp.clip(values, min=-most, max=most).astype(held_as)


def setup_inputs(seed: int = 0) -> dict:
    splits = jax.random.split(jax.random.key(seed), 8)
    q_delta = bell_draw(splits[0], (SEQUENCE_TOKENS, D), 1.0, 6.0, ((0, 16), (1, 2)))
    k_delta = bell_draw(splits[1], (SEQUENCE_TOKENS, D), 1.0, 6.0, ((0, 16), (1, 2)))
    v_delta = bell_draw(splits[2], (SEQUENCE_TOKENS, D), 1.0, 6.0, ((0, 16), (1, 2)))
    write_rate = draw_write_rate(jax.random.fold_in(splits[7], 71), 0)
    q_attn = draw_q_attn(jax.random.fold_in(splits[7], 71), 0)
    k_attn = draw_k_attn(jax.random.fold_in(splits[7], 71), 0)
    out_gain = jnp.clip(1.0 + 0.1 * jax.random.normal(splits[6], (D,), jnp.float32), 0.5, 1.5)
    return {"q_delta": q_delta, "k_delta": k_delta, "v_delta": v_delta, "write_rate": write_rate, "q_attn": q_attn, "k_attn": k_attn, "out_gain": out_gain}


highest = lax.Precision.HIGHEST

def unit_rows(entries):
    entries = entries.astype(jnp.float32)
    return entries * lax.rsqrt(lax.optimization_barrier(jnp.sum(entries * entries, axis=-1, keepdims=True)) + 1e-06)

def lower_inverse(below_part):
    length = below_part.shape[-1]
    identity = jnp.eye(length, dtype=jnp.float32)
    result = identity - below_part
    raised = below_part
    doubled = 2
    while doubled < length:
        raised = jnp.einsum('nij,njk->nik', raised, raised, precision=highest)
        result = jnp.einsum('nij,njk->nik', result, identity + raised, precision=highest)
        doubled = doubled * 2
    return result

def prepare(queries, key_rows, values, rate_rows):
    n_groups = queries.shape[0] // GROUP_TOKENS
    q_unit = unit_rows(queries).reshape(n_groups, GROUP_TOKENS, -1)
    k_unit = unit_rows(key_rows).reshape(n_groups, GROUP_TOKENS, -1)
    val_units = values.astype(jnp.float32).reshape(n_groups, GROUP_TOKENS, -1)
    rate_col = rate_rows.astype(jnp.float32).reshape(n_groups, GROUP_TOKENS, 1)
    key_inner = jnp.einsum('nik,njk->nij', k_unit, k_unit, precision=highest)
    positions = jnp.arange(GROUP_TOKENS)
    is_below = positions[:, None] > positions[None, :]
    on_or_below = positions[:, None] >= positions[None, :]
    below_part = jnp.where(is_below[None], rate_col * key_inner, 0.0)
    inverse = lower_inverse(below_part)
    writes = jnp.einsum('nij,njk->nik', inverse, rate_col * k_unit, precision=highest)
    updates = jnp.einsum('nij,njk->nik', inverse, rate_col * val_units, precision=highest)
    query_key = jnp.where(on_or_below[None], jnp.einsum('nik,njk->nij', q_unit, k_unit, precision=highest), 0.0)
    return (q_unit, k_unit, writes, updates, query_key)

def advance(carried, inputs_now):
    q_block, k_block, w_block, u_block, cross_block = inputs_now
    corrected = u_block - jnp.dot(w_block, carried, precision=highest)
    result_now = jnp.dot(q_block, carried, precision=highest) + jnp.dot(cross_block, corrected, precision=highest)
    return (carried + jnp.dot(k_block.T, corrected, precision=highest), result_now)

def delta_head(inputs_now):
    queries, key_rows, values, rate_rows = inputs_now
    q_unit, k_unit, writes, updates, query_key = prepare(queries, key_rows, values, rate_rows)
    head_size = queries.shape[-1]
    _, results = lax.scan(advance, jnp.zeros((head_size, head_size), jnp.float32), (q_unit, k_unit, writes, updates, query_key))
    return results.reshape(-1, head_size).astype(jnp.bfloat16)

def attend_head(inputs_now):
    queries, key_rows, values = inputs_now
    total_rows = queries.shape[0]
    head_size = queries.shape[-1]
    block_rows = min(512, total_rows)
    score_scale = 1.0 / math.sqrt(head_size)
    padding = jnp.zeros((WINDOW, head_size), jnp.float32)
    keys_padded = jnp.concatenate([padding, key_rows.astype(jnp.float32)], axis=0)
    values_padded = jnp.concatenate([padding, values.astype(jnp.float32)], axis=0)
    query_rows = queries.astype(jnp.float32)

    def attend_block(block_start):
        rows_now = lax.dynamic_slice_in_dim(query_rows, block_start, block_rows, 0)
        near_keys = lax.dynamic_slice_in_dim(keys_padded, block_start, WINDOW + block_rows, 0)
        near_values = lax.dynamic_slice_in_dim(values_padded, block_start, WINDOW + block_rows, 0)
        scores = jnp.dot(rows_now, near_keys.T) * score_scale
        q_index = jnp.arange(block_rows)[:, None]
        k_index = jnp.arange(WINDOW + block_rows)[None, :]
        allowed = (k_index > q_index) & (k_index <= q_index + WINDOW) & (block_start + k_index >= WINDOW)
        row_top = lax.optimization_barrier(jnp.max(jnp.where(allowed, scores, -1e+30), axis=1, keepdims=True))
        exps = jnp.exp(jnp.where(allowed, scores - row_top, -1e+30))
        weights = (exps / lax.optimization_barrier(jnp.sum(exps, axis=1, keepdims=True))).astype(jnp.bfloat16)
        return jnp.dot(weights.astype(jnp.float32), near_values)
    starts = (jnp.arange(total_rows // block_rows) * block_rows).astype(jnp.int32)
    return lax.map(attend_block, starts).reshape(total_rows, head_size)

def reference(q_delta, k_delta, v_delta, write_rate, q_attn, k_attn, out_gain):

    def by_head(entries):
        return entries.reshape(SEQUENCE_TOKENS, HEAD_COUNT, HD).transpose(1, 0, 2)
    delta_heads = lax.map(delta_head, (by_head(q_delta), by_head(k_delta), by_head(v_delta), write_rate.T))
    attended_heads = lax.map(attend_head, (by_head(q_attn), by_head(k_attn), delta_heads))
    delta_out = delta_heads.transpose(1, 0, 2).reshape(SEQUENCE_TOKENS, D)
    attended = attended_heads.transpose(1, 0, 2).reshape(SEQUENCE_TOKENS, D)
    width_mean = lax.optimization_barrier(jnp.mean(attended * attended, axis=1, keepdims=True))
    normed_out = (attended * out_gain[None, :] * lax.rsqrt(width_mean + 1e-06)).astype(jnp.bfloat16)
    return (delta_out, normed_out)
```

```python
import functools
import math

import jax
import jax.numpy as jnp
from jax import lax
from jax.experimental import pallas as pl
from jax.experimental.pallas import tpu as pltpu
from jax.sharding import PartitionSpec as P

WINDOW = 2048
HEAD = 128
PLANE = 4
F32 = jnp.float32
BF16 = jnp.bfloat16
NN = (((1,), (0,)), ((), ()))
NT = (((1,), (1,)), ((), ()))


def dot1(left, right, dims=NN):
    return lax.dot_general(left, right, dims, preferred_element_type=F32)


def split(value):
    high = value.astype(BF16)
    return high, (value - high.astype(F32)).astype(BF16)


def dot3(left, right, dims=NN):
    return (
        dot1(left[0], right[0], dims)
        + (dot1(left[0], right[1], dims) + dot1(left[1], right[0], dims))
    )


def unit_rows(entries):
    entries = entries.astype(F32)
    return entries * lax.rsqrt(jnp.sum(entries * entries, axis=-1, keepdims=True) + 1e-06)


def columns_of(head, width=HEAD):
    return pl.ds(pl.multiple_of(head * HEAD, HEAD), width)


def kernel(
    n, nh, heads, per, group, tok,
    q_ref, k_ref, v_ref, rate_ref, qa_ref, ka_ref, gain_ref,
    delta_ref, norm_ref,
    kbuf, vbuf, wbuf, scores, m_buf, c_buf, l_buf, b_buf, s_in, s_out, att, sq_out, sq_in,
    k_send, k_recv, v_send, v_recv, s_send, s_recv, sq_send, sq_recv,
):
    pos = lax.axis_index("seq")
    core = lax.axis_index("head")
    place = lax.rem(pos, PLANE)
    reach = 2 * PLANE
    chunks = heads // per
    has_up = pos + PLANE < n
    has_down = pos >= PLANE
    has_far = pos >= reach

    barrier = pltpu.get_barrier_semaphore()

    def greet(seq_index):
        pl.semaphore_signal(
            barrier, inc=1, device_id={"seq": seq_index}, device_id_type=pl.DeviceIdType.MESH
        )

    for step in range(1, PLANE):
        greet(pos - place + lax.rem(place + step, PLANE))
    for step in range(1, nh):
        pl.semaphore_signal(
            barrier, inc=1, device_id={"head": lax.rem(core + step, nh)},
            device_id_type=pl.DeviceIdType.MESH,
        )
    steps_out = jnp.logical_and(place == PLANE - 1, pos + 1 < n)
    steps_in = jnp.logical_and(place == 0, pos > 0)
    pl.when(has_up)(lambda: greet(pos + PLANE))
    pl.when(has_down)(lambda: greet(pos - PLANE))
    pl.when(steps_out)(lambda: greet(pos + 1))
    pl.when(steps_in)(lambda: greet(pos - 1))
    expected = PLANE - 1 + nh - 1
    for there in (has_up, has_down, steps_out, steps_in):
        expected = expected + there.astype(jnp.int32)
    pl.semaphore_wait(barrier, expected)

    def remote(src, dst, send_sem, recv_sem, to):
        return pltpu.make_async_remote_copy(
            src_ref=src, dst_ref=dst, send_sem=send_sem, recv_sem=recv_sem,
            device_id={"seq": to}, device_id_type=pl.DeviceIdType.MESH,
        )

    def spread(own, buf, send, recv, chunk, stage, act):
        cols = pl.ds(chunk * per * HEAD, per * HEAD)

        def one(src, index, to, reaches, cond):
            copy = remote(
                src, buf.at[reaches - 1, :, cols], send.at[index, chunk],
                recv.at[reaches - 1, chunk], to,
            )
            pl.when(cond)(lambda: act(copy))

        if stage == 0:
            src = own.at[:, cols]
            one(src, 0, pos + PLANE, PLANE, has_up)
            for step in range(1, PLANE):
                one(src, step, pos + step, step, place + step < PLANE)
        elif stage == 1:
            src = buf.at[PLANE - 1, :, cols]
            one(src, 4, pos + PLANE, reach, jnp.logical_and(has_down, has_up))
            for step in range(1, PLANE):
                one(src, 4 + step, pos + step, PLANE + step,
                    jnp.logical_and(has_down, place + step < PLANE))
                one(src, 4 + step, pos + step - PLANE, step,
                    jnp.logical_and(has_down, place + step >= PLANE))
        else:
            src = buf.at[reach - 1, :, cols]
            for step in range(1, PLANE):
                one(src, 7 + step, pos - step, reach - step,
                    jnp.logical_and(has_far, place >= step))

    def arrived(buf, recv, slot, chunk, cond):
        cols = pl.ds(chunk * per * HEAD, per * HEAD)
        here = buf.at[slot, :, cols]
        copy = pltpu.make_async_copy(here, here, recv.at[slot, chunk])
        pl.when(cond)(lambda: copy.wait())

    start = lambda copy: copy.start()
    finish = lambda copy: copy.wait_send()

    for chunk in range(chunks):
        spread(ka_ref, kbuf, k_send, k_recv, chunk, 0, start)

    for slot in range(reach):
        def clear(slot=slot):
            kbuf[slot] = jnp.zeros(kbuf.shape[1:], BF16)
            vbuf[slot] = jnp.zeros(vbuf.shape[1:], BF16)
        pl.when(pos < slot + 1)(clear)

    def clear_state():
        s_in[...] = jnp.zeros(s_in.shape, F32)
    pl.when(pos == 0)(clear_state)

    rows = lax.broadcasted_iota(jnp.int32, (tok, tok), 0)
    cols = lax.broadcasted_iota(jnp.int32, (tok, tok), 1)
    levels = tok.bit_length() - 1

    def prep(index, carry):
        apart = jnp.bitwise_xor(rows, cols)
        diagonal = (rows == cols).astype(F32)
        lane = lax.broadcasted_iota(jnp.int32, rate_ref.shape, 1)
        members = range(group)
        head_of = [index * group + i for i in members]
        q_unit = [unit_rows(q_ref[:, columns_of(h)]) for h in head_of]
        k_unit = [unit_rows(k_ref[:, columns_of(h)]) for h in head_of]
        rate = [
            jnp.sum(jnp.where(lane == h, rate_ref[...], 0.0), axis=1, keepdims=True) for h in head_of
        ]
        k_split = [split(k) for k in k_unit]
        below = [
            jnp.where(rows > cols, rate[i] * dot3(k_split[i], k_split[i], NT), 0.0) for i in members
        ]
        inverse = [diagonal - jnp.where(apart == 1, below[i], 0.0) for i in members]
        for level in range(1, levels):
            now = (apart >> level) == 1
            part = [jnp.where(now, below[i], 0.0).astype(BF16) for i in members]
            short = [inverse[i].astype(BF16) for i in members]
            inner = [dot1(part[i], short[i]).astype(BF16) for i in members]
            inverse = [inverse[i] - dot1(short[i], inner[i]) for i in members]
        rest = [
            (inverse[i] - diagonal) + dot3(split(below[i]), split(inverse[i])) for i in members
        ]
        inverse = [
            inverse[i] - dot1(inverse[i].astype(BF16), rest[i].astype(BF16)) for i in members
        ]
        targets = [
            jnp.concatenate(
                [rate[i] * k_unit[i], rate[i] * v_ref[:, columns_of(head_of[i])].astype(F32)], axis=1
            )
            for i in members
        ]
        solved = [split(dot3(split(inverse[i]), split(targets[i]))) for i in members]
        for i in members:
            h = head_of[i]
            cross = jnp.where(rows >= cols, dot3(split(q_unit[i]), k_split[i], NT), 0.0)
            mixed = dot3(split(cross), solved[i])
            l_buf[h] = q_unit[i] - mixed[:, :HEAD]
            b_buf[h] = mixed[:, HEAD:]
            moved = dot3(split(k_unit[i].T), solved[i])
            m_buf[h] = diagonal[:HEAD, :HEAD] - moved[:, :HEAD]
            c_buf[h] = moved[:, HEAD:]
        return carry

    lax.fori_loop(0, heads // group, prep, 0)

    for chunk in range(chunks):
        arrived(kbuf, k_recv, PLANE - 1, chunk, has_down)
        spread(ka_ref, kbuf, k_send, k_recv, chunk, 1, start)
    for chunk in range(chunks):
        arrived(kbuf, k_recv, reach - 1, chunk, has_far)
        spread(ka_ref, kbuf, k_send, k_recv, chunk, 2, start)

    def weigh(h, carry):
        scale = 1.0 / math.sqrt(HEAD)
        query = qa_ref[:, columns_of(h)]
        top = None
        for slot in range(reach + 1):
            keys = ka_ref[:, columns_of(h)] if slot == 0 else kbuf[slot - 1, :, columns_of(h)]
            now = dot1(query, keys, NT) * scale
            if slot == 0:
                now = jnp.where(cols <= rows, now, -1e30)
            elif slot == reach:
                now = jnp.where(jnp.logical_and(cols > rows, has_far), now, -1e30)
            else:
                now = jnp.where(pos >= slot, now, -1e30)
            scores[slot] = now
            top = now if top is None else jnp.maximum(top, now)
        top = jnp.max(top, axis=1, keepdims=True)
        total = jnp.zeros((tok, tok), F32)
        for slot in range(reach + 1):
            now = jnp.exp(scores[slot] - top)
            scores[slot] = now
            total = total + now
        scale_rows = 1.0 / jnp.sum(total, axis=1, keepdims=True)
        for slot in range(reach + 1):
            wbuf[h, slot] = (scores[slot] * scale_rows).astype(BF16)
        return carry

    late = pos >= reach + PLANE
    early_heads = jnp.where(late, heads, 0)

    def all_keys():
        for chunk in range(chunks):
            for slot in range(reach):
                if slot != PLANE - 1 and slot != reach - 1:
                    arrived(kbuf, k_recv, slot, chunk, pos >= slot + 1)

    pl.when(late)(all_keys)
    lax.fori_loop(0, early_heads, weigh, 0)

    for h in range(heads):
        state_copy = remote(s_out.at[h], s_in.at[h], s_send.at[h], s_recv.at[h], pos + 1)
        pl.when(pos > 0)(lambda: state_copy.wait_recv())
        state = split(s_in[h])

        def pass_on(h=h, state=state, state_copy=state_copy):
            s_out[h] = dot3(split(m_buf[h]), state) + c_buf[h]
            state_copy.start()
        pl.when(pos + 1 < n)(pass_on)
        delta_ref[:, columns_of(h)] = (dot3(split(l_buf[h]), state) + b_buf[h]).astype(BF16)
        if h % per == per - 1:
            spread(delta_ref, vbuf, v_send, v_recv, h // per, 0, start)

    pl.when(jnp.logical_not(late))(all_keys)
    for chunk in range(chunks):
        arrived(vbuf, v_recv, PLANE - 1, chunk, has_down)
        spread(delta_ref, vbuf, v_send, v_recv, chunk, 1, start)
    lax.fori_loop(early_heads, heads, weigh, 0)
    for chunk in range(chunks):
        arrived(vbuf, v_recv, reach - 1, chunk, has_far)
        spread(delta_ref, vbuf, v_send, v_recv, chunk, 2, start)

    squares = jnp.zeros((tok, HEAD), F32)
    for h in range(heads):
        if h % per == 0:
            for slot in range(reach):
                if slot != PLANE - 1 and slot != reach - 1:
                    arrived(vbuf, v_recv, slot, h // per, pos >= slot + 1)
        mixed = dot1(wbuf[h, 0], delta_ref[:, columns_of(h)])
        for slot in range(reach):
            mixed = mixed + dot1(wbuf[h, slot + 1], vbuf[slot, :, columns_of(h)])
        att[:, columns_of(h)] = mixed
        squares = squares + mixed * mixed
    sq_out[...] = jnp.broadcast_to(jnp.sum(squares, axis=1, keepdims=True), (tok, HEAD))
    total_sq = sq_out[...]
    trades = []
    for step in range(1, nh):
        trade = pltpu.make_async_remote_copy(
            src_ref=sq_out, dst_ref=sq_in.at[step - 1], send_sem=sq_send.at[step - 1],
            recv_sem=sq_recv.at[step - 1], device_id={"head": lax.rem(core + step, nh)},
            device_id_type=pl.DeviceIdType.MESH,
        )
        trade.start()
        trades.append(trade)
    for step, trade in enumerate(trades):
        trade.wait_recv()
        total_sq = total_sq + sq_in[step]
    scale_rows = lax.rsqrt(total_sq / (heads * HEAD * nh) + 1e-06)
    for h in range(heads):
        at = columns_of(h)
        norm_ref[:, at] = (att[:, at] * gain_ref[:, at] * scale_rows).astype(BF16)

    for trade in trades:
        trade.wait_send()
    for h in range(heads):
        state_copy = remote(s_out.at[h], s_in.at[h], s_send.at[h], s_recv.at[h], pos + 1)
        pl.when(pos + 1 < n)(lambda: state_copy.wait_send())
    for chunk in range(chunks):
        for stage in range(3):
            spread(ka_ref, kbuf, k_send, k_recv, chunk, stage, finish)
            spread(delta_ref, vbuf, v_send, v_recv, chunk, stage, finish)


def on_device(n, nh, q_delta, k_delta, v_delta, write_rate, q_attn, k_attn, out_gain):
    tok, features = q_delta.shape
    heads = write_rate.shape[1]
    per = 2 if heads % 2 == 0 else 1
    group = 4 if heads % 4 == 0 else per
    chunks = heads // per
    reach = WINDOW // tok
    assert reach == 2 * PLANE and n % PLANE == 0 and features == heads * HEAD
    vmem = pl.BlockSpec(memory_space=pltpu.VMEM)
    dma = pltpu.SemaphoreType.DMA
    return pl.pallas_call(
        functools.partial(kernel, n, nh, heads, per, group, tok),
        out_shape=[jax.ShapeDtypeStruct((tok, features), BF16)] * 2,
        in_specs=[vmem] * 7,
        out_specs=[vmem] * 2,
        scratch_shapes=[
            pltpu.VMEM((reach, tok, features), BF16),
            pltpu.VMEM((reach, tok, features), BF16),
            pltpu.VMEM((heads, reach + 1, tok, tok), BF16),
            pltpu.VMEM((reach + 1, tok, tok), F32),
            pltpu.VMEM((heads, HEAD, HEAD), F32),
            pltpu.VMEM((heads, HEAD, HEAD), F32),
            pltpu.VMEM((heads, tok, HEAD), F32),
            pltpu.VMEM((heads, tok, HEAD), F32),
            pltpu.VMEM((heads, HEAD, HEAD), F32),
            pltpu.VMEM((heads, HEAD, HEAD), F32),
            pltpu.VMEM((tok, features), F32),
            pltpu.VMEM((tok, HEAD), F32),
            pltpu.VMEM((max(nh - 1, 1), tok, HEAD), F32),
            dma((11, chunks)), dma((reach, chunks)), dma((11, chunks)), dma((reach, chunks)),
            dma((heads,)), dma((heads,)), dma((max(nh - 1, 1),)), dma((max(nh - 1, 1),)),
        ],
        compiler_params=pltpu.CompilerParams(
            collective_id=0, has_side_effects=True, vmem_limit_bytes=56 * 1024 * 1024
        ),
        cost_estimate=pl.CostEstimate(
            flops=10_000_000_000, bytes_accessed=8_000_000, transcendentals=5_000_000
        ),
    )(q_delta, k_delta, v_delta, write_rate, q_attn, k_attn, out_gain.reshape(1, features))


def solution(mesh):
    placed = (P("seq", "head"),) * 6 + (P("head"),)
    return jax.shard_map(
        functools.partial(on_device, mesh.shape["seq"], mesh.shape["head"]),
        mesh=mesh,
        in_specs=placed,
        out_specs=(P("seq", "head"), P("seq", "head")),
        check_vma=False,
    )
```

```python
import functools
import math

import jax
import jax.numpy as jnp
from jax import lax
from jax.experimental import pallas as pl
from jax.experimental.pallas import tpu as pltpu
from jax.sharding import PartitionSpec as P

WINDOW = 2048
HEAD = 128
PLANE = 4
F32 = jnp.float32
BF16 = jnp.bfloat16
NN = (((1,), (0,)), ((), ()))
NT = (((1,), (1,)), ((), ()))


def dot1(left, right, dims=NN):
    return lax.dot_general(left, right, dims, preferred_element_type=F32)


def split(value):
    high = value.astype(BF16)
    return high, (value - high.astype(F32)).astype(BF16)


def dot3(left, right, dims=NN):
    return (
        dot1(left[0], right[0], dims)
        + (dot1(left[0], right[1], dims) + dot1(left[1], right[0], dims))
    )


def unit_rows(entries):
    entries = entries.astype(F32)
    return entries * lax.rsqrt(jnp.sum(entries * entries, axis=-1, keepdims=True) + 1e-06)


def columns_of(head, width=HEAD):
    return pl.ds(pl.multiple_of(head * HEAD, HEAD), width)


def kernel(
    n, nh, heads, size, reach, unroll, tok,
    q_ref, k_ref, v_ref, rate_ref, qa_ref, ka_ref, gain_ref,
    delta_ref, norm_ref,
    parts, rates, kbuf, vbuf, wbuf, scores, m_buf, c_buf, l_buf, b_buf, s_in, s_out,
    att, att_in, sq_out, sq_in,
    in_send, in_recv, k_send, k_recv, v_send, v_recv, s_send, s_recv,
    d_send, d_recv, a_send, a_recv, sq_send, sq_recv,
):
    pos = lax.axis_index("seq")
    core = lax.axis_index("head")
    place = lax.rem(pos, size)
    base = pos - place
    mine = heads // size
    wide = mine * HEAD
    back = reach // size
    units = heads
    has_up = pos + size < n
    has_down = pos >= size
    own_cols = pl.ds(pl.multiple_of(place * wide, HEAD), wide)

    barrier = pltpu.get_barrier_semaphore()

    def greet(seq_index):
        pl.semaphore_signal(
            barrier, inc=1, device_id={"seq": seq_index}, device_id_type=pl.DeviceIdType.MESH
        )

    for step in range(1, size):
        greet(base + lax.rem(place + step, size))
    for step in range(1, nh):
        pl.semaphore_signal(
            barrier, inc=1, device_id={"head": lax.rem(core + step, nh)},
            device_id_type=pl.DeviceIdType.MESH,
        )
    pl.when(has_up)(lambda: greet(pos + size))
    pl.when(has_down)(lambda: greet(pos - size))
    pl.semaphore_wait(
        barrier, size - 1 + nh - 1 + has_up.astype(jnp.int32) + has_down.astype(jnp.int32)
    )

    def remote(src, dst, send_sem, recv_sem, to):
        return pltpu.make_async_remote_copy(
            src_ref=src, dst_ref=dst, send_sem=send_sem, recv_sem=recv_sem,
            device_id={"seq": to}, device_id_type=pl.DeviceIdType.MESH,
        )

    def peer(step):
        return lax.rem(place + step, size)

    def deal(which, step):
        to = peer(step)
        if which == 5:
            src, dst = rate_ref, rates.at[place]
        else:
            ref = (k_ref, q_ref, v_ref, ka_ref, qa_ref)[which]
            src = ref.at[:, pl.ds(pl.multiple_of(to * wide, HEAD), wide)]
            dst = kbuf.at[reach + place] if which == 3 else parts.at[which, place]
        return remote(src, dst, in_send.at[which, step], in_recv.at[which, step], base + to)

    for which in (5, 0, 1, 2, 3, 4):
        for step in range(1, size):
            deal(which, step).start()
    rates[place] = rate_ref[...]
    for which, ref in enumerate((k_ref, q_ref, v_ref, ka_ref, qa_ref)):
        if which == 3:
            kbuf[reach + place] = ref[:, own_cols]
        else:
            parts[which, place] = ref[:, own_cols]

    def up(buf, send, recv, r, j):
        at = (back - r) * size + j
        return remote(
            buf.at[at], buf.at[at - size], send.at[r, j], recv.at[r, j], pos + size
        )

    def send_up(buf, send, recv, r, j):
        pl.when(jnp.logical_and(has_up, pos >= r * size))(
            lambda: up(buf, send, recv, r, j).start()
        )

    def arrived(buf, send, recv, r, j):
        pl.when(pos >= r * size)(lambda: up(buf, send, recv, r - 1, j).wait_recv())

    for r in range(1, back + 1):
        def clear(r=r):
            for j in range(size):
                kbuf[(back - r) * size + j] = jnp.zeros(kbuf.shape[1:], BF16)
                vbuf[(back - r) * size + j] = jnp.zeros(vbuf.shape[1:], BF16)
        pl.when(pos < r * size)(clear)

    def clear_state():
        s_in[...] = jnp.zeros(s_in.shape, F32)
    pl.when(jnp.logical_not(has_down))(clear_state)

    for which in (5, 0, 1, 2):
        for step in range(1, size):
            deal(which, step).wait_recv()

    rows = lax.broadcasted_iota(jnp.int32, (tok, tok), 0)
    cols = lax.broadcasted_iota(jnp.int32, (tok, tok), 1)
    levels = tok.bit_length() - 1

    def prep(index, carry):
        apart = jnp.bitwise_xor(rows, cols)
        diagonal = (rows == cols).astype(F32)
        lane = lax.broadcasted_iota(jnp.int32, rate_ref.shape, 1)
        members = range(unroll)
        unit_of = [index * unroll + i for i in members]
        block_of = [u // mine for u in unit_of]
        head_of = [lax.rem(u, mine) for u in unit_of]
        q_unit = [unit_rows(parts[1, block_of[i], :, columns_of(head_of[i])]) for i in members]
        k_unit = [unit_rows(parts[0, block_of[i], :, columns_of(head_of[i])]) for i in members]
        rate = [
            jnp.sum(
                jnp.where(lane == place * mine + head_of[i], rates[block_of[i]], 0.0),
                axis=1, keepdims=True,
            )
            for i in members
        ]
        k_split = [split(k) for k in k_unit]
        below = [
            jnp.where(rows > cols, rate[i] * dot3(k_split[i], k_split[i], NT), 0.0) for i in members
        ]
        inverse = [diagonal - jnp.where(apart == 1, below[i], 0.0) for i in members]
        for level in range(1, levels):
            now = (apart >> level) == 1
            part = [jnp.where(now, below[i], 0.0).astype(BF16) for i in members]
            short = [inverse[i].astype(BF16) for i in members]
            inner = [dot1(part[i], short[i]).astype(BF16) for i in members]
            inverse = [inverse[i] - dot1(short[i], inner[i]) for i in members]
        rest = [
            (inverse[i] - diagonal) + dot3(split(below[i]), split(inverse[i])) for i in members
        ]
        inverse = [
            inverse[i] - dot1(inverse[i].astype(BF16), rest[i].astype(BF16)) for i in members
        ]
        targets = [
            jnp.concatenate(
                [rate[i] * k_unit[i], rate[i] * parts[2, block_of[i], :, columns_of(head_of[i])].astype(F32)], axis=1
            )
            for i in members
        ]
        solved = [split(dot3(split(inverse[i]), split(targets[i]))) for i in members]
        for i in members:
            h = unit_of[i]
            cross = jnp.where(rows >= cols, dot3(split(q_unit[i]), k_split[i], NT), 0.0)
            mixed = dot3(split(cross), solved[i])
            l_buf[h] = q_unit[i] - mixed[:, :HEAD]
            b_buf[h] = mixed[:, HEAD:]
            moved = dot3(split(k_unit[i].T), solved[i])
            m_buf[h] = diagonal[:HEAD, :HEAD] - moved[:, :HEAD]
            c_buf[h] = moved[:, HEAD:]

        def keys_on():
            for step in range(1, size):
                deal(3, step).wait_recv()
            for j in range(size):
                send_up(kbuf, k_send, k_recv, 0, j)
        pl.when(index == 0)(keys_on)
        return carry

    lax.fori_loop(0, units // unroll, prep, 0)

    for step in range(1, size):
        deal(4, step).wait_recv()

    def weigh(h, carry):
        scale = 1.0 / math.sqrt(HEAD)
        block = h // mine
        at = columns_of(lax.rem(h, mine))
        query = parts[4, block, :, at]
        top = None
        for slot in range(reach + 1):
            keys = kbuf[reach + block - slot, :, at]
            now = dot1(query, keys, NT) * scale
            if slot == 0:
                now = jnp.where(cols <= rows, now, -1e30)
            elif slot == reach:
                now = jnp.where(jnp.logical_and(cols > rows, base + block >= slot), now, -1e30)
            else:
                now = jnp.where(base + block >= slot, now, -1e30)
            scores[slot] = now
            top = now if top is None else jnp.maximum(top, now)
        top = jnp.max(top, axis=1, keepdims=True)
        total = jnp.zeros((tok, tok), F32)
        for slot in range(reach + 1):
            now = jnp.exp(scores[slot] - top)
            scores[slot] = now
            total = total + now
        scale_rows = 1.0 / jnp.sum(total, axis=1, keepdims=True)
        for slot in range(reach + 1):
            wbuf[h, slot] = (scores[slot] * scale_rows).astype(BF16)
        return carry

    def state_copy(i):
        return remote(s_out.at[i], s_in.at[i], s_send.at[i], s_recv.at[i], pos + size)

    for i in range(mine):
        pl.when(has_down)(lambda: state_copy(i).wait_recv())
        state = s_in[i]
        states = []
        for j in range(size):
            states.append(split(state))
            state = dot3(split(m_buf[j * mine + i]), states[-1]) + c_buf[j * mine + i]
        s_out[i] = state
        pl.when(has_up)(lambda: state_copy(i).start())
        for j in range(size):
            u = j * mine + i
            vbuf[reach + j, :, i * HEAD:(i + 1) * HEAD] = (
                dot3(split(l_buf[u]), states[j]) + b_buf[u]
            ).astype(BF16)
    for j in range(size):
        send_up(vbuf, v_send, v_recv, 0, j)

    def give_delta(step):
        to = peer(step)
        return remote(
            vbuf.at[reach + to], delta_ref.at[:, own_cols], d_send.at[step], d_recv.at[step],
            base + to,
        )

    for step in range(1, size):
        give_delta(step).start()
    delta_ref[:, own_cols] = vbuf[reach + place]

    for r in range(1, back + 1):
        for j in range(size):
            arrived(kbuf, k_send, k_recv, r, j)
            if r < back:
                send_up(kbuf, k_send, k_recv, r, j)
    half = units // 2
    lax.fori_loop(0, half, weigh, 0)
    for r in range(1, back):
        for j in range(size):
            arrived(vbuf, v_send, v_recv, r, j)
            send_up(vbuf, v_send, v_recv, r, j)
    lax.fori_loop(half, units, weigh, 0)
    for j in range(size):
        arrived(vbuf, v_send, v_recv, back, j)

    def give_att(step):
        to = peer(step)
        return remote(
            att.at[to], att_in.at[place], a_send.at[step], a_recv.at[step], base + to
        )

    def mix(step, carry):
        block = lax.rem(place + step, size)
        for i in range(mine):
            at = slice(i * HEAD, (i + 1) * HEAD)
            mixed = jnp.zeros((tok, HEAD), F32)
            for slot in range(reach + 1):
                mixed = mixed + dot1(
                    wbuf[block * mine + i, slot], vbuf[reach + block - slot, :, at]
                )
            att[block, :, at] = mixed.astype(BF16)
        return carry

    for step in range(1, size):
        mix(step, 0)
        give_att(step).start()
    mix(0, 0)
    att_in[place] = att[place]
    for step in range(1, size):
        give_att(step).wait_recv()

    squares = jnp.zeros((tok, wide), F32)
    for j in range(size):
        now = att_in[j].astype(F32)
        squares = squares + now * now
    sq_out[...] = jnp.broadcast_to(jnp.sum(squares, axis=1, keepdims=True), (tok, HEAD))
    total_sq = sq_out[...]
    trades = []
    for step in range(1, nh):
        trade = pltpu.make_async_remote_copy(
            src_ref=sq_out, dst_ref=sq_in.at[step - 1], send_sem=sq_send.at[step - 1],
            recv_sem=sq_recv.at[step - 1], device_id={"head": lax.rem(core + step, nh)},
            device_id_type=pl.DeviceIdType.MESH,
        )
        trade.start()
        trades.append(trade)
    for step, trade in enumerate(trades):
        trade.wait_recv()
        total_sq = total_sq + sq_in[step]
    scale_rows = lax.rsqrt(total_sq / (heads * HEAD * nh) + 1e-06)
    for j in range(size):
        for i in range(mine):
            at = slice((j * mine + i) * HEAD, (j * mine + i + 1) * HEAD)
            now = att_in[j, :, i * HEAD:(i + 1) * HEAD].astype(F32)
            norm_ref[:, at] = (now * gain_ref[:, at] * scale_rows).astype(BF16)

    for trade in trades:
        trade.wait_send()
    for step in range(1, size):
        give_delta(step).wait()
        give_att(step).wait_send()
        for which in range(6):
            deal(which, step).wait_send()

    def sent_up():
        for i in range(mine):
            state_copy(i).wait_send()
        for r in range(back):
            for j in range(size):
                pl.when(pos >= r * size)(lambda: up(kbuf, k_send, k_recv, r, j).wait_send())
                pl.when(pos >= r * size)(lambda: up(vbuf, v_send, v_recv, r, j).wait_send())
    pl.when(has_up)(sent_up)


def on_device(n, nh, q_delta, k_delta, v_delta, write_rate, q_attn, k_attn, out_gain):
    tok, features = q_delta.shape
    heads = write_rate.shape[1]
    size = PLANE
    while heads % size or n % size:
        size //= 2
    mine = heads // size
    wide = mine * HEAD
    unroll = 4 if heads % 4 == 0 else 1
    reach = WINDOW // tok
    back = reach // size
    assert reach % size == 0 and features == heads * HEAD
    vmem = pl.BlockSpec(memory_space=pltpu.VMEM)
    dma = pltpu.SemaphoreType.DMA
    return pl.pallas_call(
        functools.partial(kernel, n, nh, heads, size, reach, unroll, tok),
        out_shape=[jax.ShapeDtypeStruct((tok, features), BF16)] * 2,
        in_specs=[vmem] * 7,
        out_specs=[vmem] * 2,
        scratch_shapes=[
            pltpu.VMEM((5, size, tok, wide), BF16),
            pltpu.VMEM((size, tok, heads), F32),
            pltpu.VMEM((reach + size, tok, wide), BF16),
            pltpu.VMEM((reach + size, tok, wide), BF16),
            pltpu.VMEM((heads, reach + 1, tok, tok), BF16),
            pltpu.VMEM((reach + 1, tok, tok), F32),
            pltpu.VMEM((heads, HEAD, HEAD), F32),
            pltpu.VMEM((heads, HEAD, HEAD), F32),
            pltpu.VMEM((heads, tok, HEAD), F32),
            pltpu.VMEM((heads, tok, HEAD), F32),
            pltpu.VMEM((mine, HEAD, HEAD), F32),
            pltpu.VMEM((mine, HEAD, HEAD), F32),
            pltpu.VMEM((size, tok, wide), BF16),
            pltpu.VMEM((size, tok, wide), BF16),
            pltpu.VMEM((tok, HEAD), F32),
            pltpu.VMEM((max(nh - 1, 1), tok, HEAD), F32),
            dma((6, size)), dma((6, size)),
            dma((back, size)), dma((back, size)), dma((back, size)), dma((back, size)),
            dma((mine,)), dma((mine,)), dma((size,)), dma((size,)), dma((size,)), dma((size,)),
            dma((max(nh - 1, 1),)), dma((max(nh - 1, 1),)),
        ],
        compiler_params=pltpu.CompilerParams(
            collective_id=0, has_side_effects=True, vmem_limit_bytes=56 * 1024 * 1024
        ),
        cost_estimate=pl.CostEstimate(
            flops=10_000_000_000, bytes_accessed=8_000_000, transcendentals=5_000_000
        ),
    )(q_delta, k_delta, v_delta, write_rate, q_attn, k_attn, out_gain.reshape(1, features))


def solution(mesh):
    placed = (P("seq", "head"),) * 6 + (P("head"),)
    return jax.shard_map(
        functools.partial(on_device, mesh.shape["seq"], mesh.shape["head"]),
        mesh=mesh,
        in_specs=placed,
        out_specs=(P("seq", "head"), P("seq", "head")),
        check_vma=False,
    )
```

```python
import functools
import math

import jax
import jax.numpy as jnp
from jax import lax
from jax.experimental import pallas as pl
from jax.experimental.pallas import tpu as pltpu
from jax.sharding import PartitionSpec as P

WINDOW = 2048
HEAD = 128
PLANE = 4
F32 = jnp.float32
BF16 = jnp.bfloat16
NN = (((1,), (0,)), ((), ()))
NT = (((1,), (1,)), ((), ()))


def dot1(left, right, dims=NN):
    return lax.dot_general(left, right, dims, preferred_element_type=F32)


def split(value):
    high = value.astype(BF16)
    return high, (value - high.astype(F32)).astype(BF16)


def dot3(left, right, dims=NN):
    return (
        dot1(left[0], right[0], dims)
        + (dot1(left[0], right[1], dims) + dot1(left[1], right[0], dims))
    )


def unit_rows(entries):
    entries = entries.astype(F32)
    return entries * lax.rsqrt(jnp.sum(entries * entries, axis=-1, keepdims=True) + 1e-06)


def columns_of(head, width=HEAD):
    return pl.ds(pl.multiple_of(head * HEAD, HEAD), width)


def kernel(
    n, nh, heads, size, reach, unroll, tok,
    q_ref, k_ref, v_ref, rate_ref, qa_ref, ka_ref, gain_ref,
    delta_ref, norm_ref,
    parts, rates, kbuf, vbuf, wbuf, scores, m_buf, c_buf, l_buf, b_buf, s_in, s_out, t_buf,
    att, att_in, sq_out, sq_in,
    in_send, in_recv, k_send, k_recv, v_send, v_recv, s_send, s_recv,
    d_send, d_recv, a_send, a_recv, sq_send, sq_recv,
):
    pos = lax.axis_index("seq")
    core = lax.axis_index("head")
    place = lax.rem(pos, size)
    base = pos - place
    mine = heads // size
    wide = mine * HEAD
    back = reach // size
    units = heads
    has_up = pos + size < n
    has_down = pos >= size
    own_cols = pl.ds(pl.multiple_of(place * wide, HEAD), wide)

    barrier = pltpu.get_barrier_semaphore()

    def greet(seq_index):
        pl.semaphore_signal(
            barrier, inc=1, device_id={"seq": seq_index}, device_id_type=pl.DeviceIdType.MESH
        )

    for step in range(1, size):
        greet(base + lax.rem(place + step, size))
    for step in range(1, nh):
        pl.semaphore_signal(
            barrier, inc=1, device_id={"head": lax.rem(core + step, nh)},
            device_id_type=pl.DeviceIdType.MESH,
        )
    pl.when(has_up)(lambda: greet(pos + size))
    pl.when(has_down)(lambda: greet(pos - size))
    pl.semaphore_wait(
        barrier, size - 1 + nh - 1 + has_up.astype(jnp.int32) + has_down.astype(jnp.int32)
    )

    def remote(src, dst, send_sem, recv_sem, to):
        return pltpu.make_async_remote_copy(
            src_ref=src, dst_ref=dst, send_sem=send_sem, recv_sem=recv_sem,
            device_id={"seq": to}, device_id_type=pl.DeviceIdType.MESH,
        )

    def peer(step):
        return lax.rem(place + step, size)

    def deal(which, step):
        to = peer(step)
        if which == 5:
            src, dst = rate_ref, rates.at[place]
        else:
            ref = (k_ref, q_ref, v_ref, ka_ref, qa_ref)[which]
            src = ref.at[:, pl.ds(pl.multiple_of(to * wide, HEAD), wide)]
            dst = kbuf.at[reach + place] if which == 3 else parts.at[which, place]
        return remote(src, dst, in_send.at[which, step], in_recv.at[which, step], base + to)

    for step in range(1, size):
        for which in (5, 0, 1, 2):
            deal(which, step).start()
    rates[place] = rate_ref[...]
    for which, ref in enumerate((k_ref, q_ref, v_ref, ka_ref, qa_ref)):
        if which == 3:
            kbuf[reach + place] = ref[:, own_cols]
        else:
            parts[which, place] = ref[:, own_cols]

    def up(buf, send, recv, r, j):
        at = (back - r) * size + j
        return remote(
            buf.at[at], buf.at[at - size], send.at[r, j], recv.at[r, j], pos + size
        )

    def send_up(buf, send, recv, r, j):
        pl.when(jnp.logical_and(has_up, pos >= r * size))(
            lambda: up(buf, send, recv, r, j).start()
        )

    def arrived(buf, send, recv, r, j):
        pl.when(pos >= r * size)(lambda: up(buf, send, recv, r - 1, j).wait_recv())

    for r in range(1, back + 1):
        def clear(r=r):
            for j in range(size):
                kbuf[(back - r) * size + j] = jnp.zeros(kbuf.shape[1:], BF16)
                vbuf[(back - r) * size + j] = jnp.zeros(vbuf.shape[1:], BF16)
        pl.when(pos < r * size)(clear)

    def clear_state():
        s_in[...] = jnp.zeros(s_in.shape, F32)
    pl.when(jnp.logical_not(has_down))(clear_state)

    first = unroll // mine
    for step in range(1, first):
        for which in (5, 0, 1, 2):
            deal(which, step).wait_recv()
    for which in (3, 4):
        for step in range(1, size):
            deal(which, step).start()

    rows = lax.broadcasted_iota(jnp.int32, (tok, tok), 0)
    cols = lax.broadcasted_iota(jnp.int32, (tok, tok), 1)
    levels = tok.bit_length() - 1

    def prep(index, carry):
        apart = jnp.bitwise_xor(rows, cols)
        diagonal = (rows == cols).astype(F32)
        lane = lax.broadcasted_iota(jnp.int32, rate_ref.shape, 1)
        members = range(unroll)
        turn_of = [index * unroll + i for i in members]
        head_of = [lax.rem(u, mine) for u in turn_of]
        block_of = [lax.rem(place - u // mine + size, size) for u in turn_of]
        unit_of = [block_of[i] * mine + head_of[i] for i in members]
        q_unit = [unit_rows(parts[1, block_of[i], :, columns_of(head_of[i])]) for i in members]
        k_unit = [unit_rows(parts[0, block_of[i], :, columns_of(head_of[i])]) for i in members]
        rate = [
            jnp.sum(
                jnp.where(lane == place * mine + head_of[i], rates[block_of[i]], 0.0),
                axis=1, keepdims=True,
            )
            for i in members
        ]
        k_split = [split(k) for k in k_unit]
        below = [
            jnp.where(rows > cols, rate[i] * dot3(k_split[i], k_split[i], NT), 0.0) for i in members
        ]
        inverse = [diagonal - jnp.where(apart == 1, below[i], 0.0) for i in members]
        for level in range(1, levels):
            now = (apart >> level) == 1
            part = [jnp.where(now, below[i], 0.0).astype(BF16) for i in members]
            short = [inverse[i].astype(BF16) for i in members]
            inner = [dot1(part[i], short[i]).astype(BF16) for i in members]
            inverse = [inverse[i] - dot1(short[i], inner[i]) for i in members]
        rest = [
            (inverse[i] - diagonal) + dot3(split(below[i]), split(inverse[i])) for i in members
        ]
        inverse = [
            inverse[i] - dot1(inverse[i].astype(BF16), rest[i].astype(BF16)) for i in members
        ]
        targets = [
            jnp.concatenate(
                [rate[i] * k_unit[i], rate[i] * parts[2, block_of[i], :, columns_of(head_of[i])].astype(F32)], axis=1
            )
            for i in members
        ]
        solved = [split(dot3(split(inverse[i]), split(targets[i]))) for i in members]
        for i in members:
            h = unit_of[i]
            cross = jnp.where(rows >= cols, dot3(split(q_unit[i]), k_split[i], NT), 0.0)
            mixed = dot3(split(cross), solved[i])
            l_buf[h] = q_unit[i] - mixed[:, :HEAD]
            b_buf[h] = mixed[:, HEAD:]
            moved = dot3(split(k_unit[i].T), solved[i])
            m_buf[h] = diagonal[:HEAD, :HEAD] - moved[:, :HEAD]
            c_buf[h] = moved[:, HEAD:]

        def keys_on():
            for step in range(first, size):
                for which in (5, 0, 1, 2):
                    deal(which, step).wait_recv()
            for step in range(1, size):
                deal(3, step).wait_recv()
            for j in range(size):
                send_up(kbuf, k_send, k_recv, 0, j)
        pl.when(index == 0)(keys_on)
        return carry

    lax.fori_loop(0, units // unroll, prep, 0)

    for step in range(1, size):
        deal(4, step).wait_recv()

    def weigh(h, carry):
        scale = 1.0 / math.sqrt(HEAD)
        h = units - 1 - h
        block = h // mine
        at = columns_of(lax.rem(h, mine))
        query = parts[4, block, :, at]
        top = None
        for slot in range(reach + 1):
            keys = kbuf[reach + block - slot, :, at]
            now = dot1(query, keys, NT) * scale
            if slot == 0:
                now = jnp.where(cols <= rows, now, -1e30)
            elif slot == reach:
                now = jnp.where(jnp.logical_and(cols > rows, base + block >= slot), now, -1e30)
            else:
                now = jnp.where(base + block >= slot, now, -1e30)
            scores[slot] = now
            top = now if top is None else jnp.maximum(top, now)
        top = jnp.max(top, axis=1, keepdims=True)
        total = jnp.zeros((tok, tok), F32)
        for slot in range(reach + 1):
            now = jnp.exp(scores[slot] - top)
            scores[slot] = now
            total = total + now
        scale_rows = 1.0 / jnp.sum(total, axis=1, keepdims=True)
        for slot in range(reach + 1):
            wbuf[h, slot] = (scores[slot] * scale_rows).astype(BF16)
        return carry

    def state_copy(i):
        return remote(s_out.at[i], s_in.at[i], s_send.at[i], s_recv.at[i], pos + size)

    whole = [jnp.concatenate([m_buf[i], c_buf[i]], axis=1) for i in range(mine)]
    for j in range(1, size):
        for i in range(mine):
            u = j * mine + i
            moved = dot3(split(m_buf[u]), split(whole[i]))
            whole[i] = jnp.concatenate([moved[:, :HEAD], moved[:, HEAD:] + c_buf[u]], axis=1)
    for i in range(mine):
        t_buf[i] = whole[i]

    for r in range(1, back):
        for j in range(size):
            arrived(kbuf, k_send, k_recv, r, j)
            send_up(kbuf, k_send, k_recv, r, j)

    last = jnp.logical_and(has_down, jnp.logical_not(has_up))
    some = jnp.where(pos >= reach, units // 4, 0)
    early = jnp.where(last, units, some)

    def far_keys():
        for j in range(size):
            arrived(kbuf, k_send, k_recv, back, j)

    pl.when(early > 0)(far_keys)
    lax.fori_loop(0, early, weigh, 0)

    for i in range(mine):
        pl.when(has_down)(lambda: state_copy(i).wait_recv())
        s_out[i] = dot3(split(t_buf[i, :, :HEAD]), split(s_in[i])) + t_buf[i, :, HEAD:]
        pl.when(has_up)(lambda: state_copy(i).start())
    state = [s_in[i] for i in range(mine)]
    for j in range(size):
        for i in range(mine):
            u = j * mine + i
            now = split(state[i])
            vbuf[reach + j, :, i * HEAD:(i + 1) * HEAD] = (
                dot3(split(l_buf[u]), now) + b_buf[u]
            ).astype(BF16)
            if j + 1 < size:
                state[i] = dot3(split(m_buf[u]), now) + c_buf[u]
    for j in range(size):
        send_up(vbuf, v_send, v_recv, 0, j)

    def give_delta(step):
        to = peer(step)
        return remote(
            vbuf.at[reach + to], delta_ref.at[:, own_cols], d_send.at[step], d_recv.at[step],
            base + to,
        )

    for step in range(1, size):
        give_delta(step).start()
    delta_ref[:, own_cols] = vbuf[reach + place]

    pl.when(early == 0)(far_keys)
    half = early + (units - early) // 2
    lax.fori_loop(early, half, weigh, 0)
    for r in range(1, back):
        for j in range(size):
            arrived(vbuf, v_send, v_recv, r, j)
            send_up(vbuf, v_send, v_recv, r, j)
    lax.fori_loop(half, units, weigh, 0)
    for j in range(size):
        arrived(vbuf, v_send, v_recv, back, j)

    def give_att(step):
        to = peer(step)
        return remote(
            att.at[to], att_in.at[place], a_send.at[step], a_recv.at[step], base + to
        )

    def mix(step, carry):
        block = lax.rem(place + step, size)
        for i in range(mine):
            at = slice(i * HEAD, (i + 1) * HEAD)
            mixed = jnp.zeros((tok, HEAD), F32)
            for slot in range(reach + 1):
                mixed = mixed + dot1(
                    wbuf[block * mine + i, slot], vbuf[reach + block - slot, :, at]
                )
            att[block, :, at] = mixed.astype(BF16)
        return carry

    for step in range(1, size):
        mix(step, 0)
        give_att(step).start()
    mix(0, 0)
    att_in[place] = att[place]
    for step in range(1, size):
        give_att(step).wait_recv()

    squares = jnp.zeros((tok, wide), F32)
    for j in range(size):
        now = att_in[j].astype(F32)
        squares = squares + now * now
    sq_out[...] = jnp.broadcast_to(jnp.sum(squares, axis=1, keepdims=True), (tok, HEAD))
    total_sq = sq_out[...]
    trades = []
    for step in range(1, nh):
        trade = pltpu.make_async_remote_copy(
            src_ref=sq_out, dst_ref=sq_in.at[step - 1], send_sem=sq_send.at[step - 1],
            recv_sem=sq_recv.at[step - 1], device_id={"head": lax.rem(core + step, nh)},
            device_id_type=pl.DeviceIdType.MESH,
        )
        trade.start()
        trades.append(trade)
    for step, trade in enumerate(trades):
        trade.wait_recv()
        total_sq = total_sq + sq_in[step]
    scale_rows = lax.rsqrt(total_sq / (heads * HEAD * nh) + 1e-06)
    for j in range(size):
        for i in range(mine):
            at = slice((j * mine + i) * HEAD, (j * mine + i + 1) * HEAD)
            now = att_in[j, :, i * HEAD:(i + 1) * HEAD].astype(F32)
            norm_ref[:, at] = (now * gain_ref[:, at] * scale_rows).astype(BF16)

    for trade in trades:
        trade.wait_send()
    for step in range(1, size):
        give_delta(step).wait()
        give_att(step).wait_send()
        for which in range(6):
            deal(which, step).wait_send()

    def sent_up():
        for i in range(mine):
            state_copy(i).wait_send()
        for r in range(back):
            for j in range(size):
                pl.when(pos >= r * size)(lambda: up(kbuf, k_send, k_recv, r, j).wait_send())
                pl.when(pos >= r * size)(lambda: up(vbuf, v_send, v_recv, r, j).wait_send())
    pl.when(has_up)(sent_up)


def on_device(n, nh, q_delta, k_delta, v_delta, write_rate, q_attn, k_attn, out_gain):
    tok, features = q_delta.shape
    heads = write_rate.shape[1]
    size = PLANE
    while heads % size or n % size:
        size //= 2
    mine = heads // size
    wide = mine * HEAD
    unroll = 4 if heads % 4 == 0 else 1
    reach = WINDOW // tok
    back = reach // size
    assert reach % size == 0 and features == heads * HEAD
    vmem = pl.BlockSpec(memory_space=pltpu.VMEM)
    dma = pltpu.SemaphoreType.DMA
    return pl.pallas_call(
        functools.partial(kernel, n, nh, heads, size, reach, unroll, tok),
        out_shape=[jax.ShapeDtypeStruct((tok, features), BF16)] * 2,
        in_specs=[vmem] * 7,
        out_specs=[vmem] * 2,
        scratch_shapes=[
            pltpu.VMEM((5, size, tok, wide), BF16),
            pltpu.VMEM((size, tok, heads), F32),
            pltpu.VMEM((reach + size, tok, wide), BF16),
            pltpu.VMEM((reach + size, tok, wide), BF16),
            pltpu.VMEM((heads, reach + 1, tok, tok), BF16),
            pltpu.VMEM((reach + 1, tok, tok), F32),
            pltpu.VMEM((heads, HEAD, HEAD), F32),
            pltpu.VMEM((heads, HEAD, HEAD), F32),
            pltpu.VMEM((heads, tok, HEAD), F32),
            pltpu.VMEM((heads, tok, HEAD), F32),
            pltpu.VMEM((mine, HEAD, HEAD), F32),
            pltpu.VMEM((mine, HEAD, HEAD), F32),
            pltpu.VMEM((mine, HEAD, 2 * HEAD), F32),
            pltpu.VMEM((size, tok, wide), BF16),
            pltpu.VMEM((size, tok, wide), BF16),
            pltpu.VMEM((tok, HEAD), F32),
            pltpu.VMEM((max(nh - 1, 1), tok, HEAD), F32),
            dma((6, size)), dma((6, size)),
            dma((back, size)), dma((back, size)), dma((back, size)), dma((back, size)),
            dma((mine,)), dma((mine,)), dma((size,)), dma((size,)), dma((size,)), dma((size,)),
            dma((max(nh - 1, 1),)), dma((max(nh - 1, 1),)),
        ],
        compiler_params=pltpu.CompilerParams(
            collective_id=0, has_side_effects=True, vmem_limit_bytes=56 * 1024 * 1024
        ),
        cost_estimate=pl.CostEstimate(
            flops=10_000_000_000, bytes_accessed=8_000_000, transcendentals=5_000_000
        ),
    )(q_delta, k_delta, v_delta, write_rate, q_attn, k_attn, out_gain.reshape(1, features))


def solution(mesh):
    placed = (P("seq", "head"),) * 6 + (P("head"),)
    return jax.shard_map(
        functools.partial(on_device, mesh.shape["seq"], mesh.shape["head"]),
        mesh=mesh,
        in_specs=placed,
        out_specs=(P("seq", "head"), P("seq", "head")),
        check_vma=False,
    )
```

```python
import functools
import math

import jax
import jax.numpy as jnp
from jax import lax
from jax.experimental import pallas as pl
from jax.experimental.pallas import tpu as pltpu
from jax.sharding import PartitionSpec as P

WINDOW = 2048
HEAD = 128
PLANE = 4
F32 = jnp.float32
BF16 = jnp.bfloat16
NN = (((1,), (0,)), ((), ()))
NT = (((1,), (1,)), ((), ()))


def dot1(left, right, dims=NN):
    return lax.dot_general(left, right, dims, preferred_element_type=F32)


def split(value):
    high = value.astype(BF16)
    return high, (value - high.astype(F32)).astype(BF16)


def dot3(left, right, dims=NN):
    return (
        dot1(left[0], right[0], dims)
        + (dot1(left[0], right[1], dims) + dot1(left[1], right[0], dims))
    )


def unit_rows(entries):
    entries = entries.astype(F32)
    return entries * lax.rsqrt(jnp.sum(entries * entries, axis=-1, keepdims=True) + 1e-06)


def columns_of(head, width=HEAD):
    return pl.ds(pl.multiple_of(head * HEAD, HEAD), width)


def kernel(
    n, nh, heads, size, reach, unroll, tok,
    q_ref, k_ref, v_ref, rate_ref, qa_ref, ka_ref, gain_ref,
    delta_ref, norm_ref,
    parts, rates, kbuf, vbuf, wbuf, scores, m_buf, c_buf, l_buf, b_buf, s_in, s_out, t_buf,
    att, att_in, sq_out, sq_in,
    in_send, in_recv, k_send, k_recv, v_send, v_recv, s_send, s_recv,
    d_send, d_recv, a_send, a_recv, sq_send, sq_recv,
):
    pos = lax.axis_index("seq")
    core = lax.axis_index("head")
    place = lax.rem(pos, size)
    base = pos - place
    mine = heads // size
    wide = mine * HEAD
    back = reach // size
    units = heads
    has_up = pos + size < n
    has_down = pos >= size
    own_cols = pl.ds(pl.multiple_of(place * wide, HEAD), wide)

    barrier = pltpu.get_barrier_semaphore()

    def greet(seq_index):
        pl.semaphore_signal(
            barrier, inc=1, device_id={"seq": seq_index}, device_id_type=pl.DeviceIdType.MESH
        )

    for step in range(1, size):
        greet(base + lax.rem(place + step, size))
    for step in range(1, nh):
        pl.semaphore_signal(
            barrier, inc=1, device_id={"head": lax.rem(core + step, nh)},
            device_id_type=pl.DeviceIdType.MESH,
        )
    pl.when(has_up)(lambda: greet(pos + size))
    pl.when(has_down)(lambda: greet(pos - size))
    pl.semaphore_wait(
        barrier, size - 1 + nh - 1 + has_up.astype(jnp.int32) + has_down.astype(jnp.int32)
    )

    def remote(src, dst, send_sem, recv_sem, to):
        return pltpu.make_async_remote_copy(
            src_ref=src, dst_ref=dst, send_sem=send_sem, recv_sem=recv_sem,
            device_id={"seq": to}, device_id_type=pl.DeviceIdType.MESH,
        )

    def peer(step):
        return lax.rem(place + step, size)

    def deal(which, step):
        to = peer(step)
        if which == 5:
            src, dst = rate_ref, rates.at[place]
        else:
            ref = (k_ref, q_ref, v_ref, ka_ref, qa_ref)[which]
            src = ref.at[:, pl.ds(pl.multiple_of(to * wide, HEAD), wide)]
            dst = kbuf.at[reach + place] if which == 3 else parts.at[which, place]
        return remote(src, dst, in_send.at[which, step], in_recv.at[which, step], base + to)

    for step in range(1, size):
        for which in (5, 0, 1, 2):
            deal(which, step).start()
    rates[place] = rate_ref[...]
    for which, ref in enumerate((k_ref, q_ref, v_ref, ka_ref, qa_ref)):
        if which == 3:
            kbuf[reach + place] = ref[:, own_cols]
        else:
            parts[which, place] = ref[:, own_cols]

    def up(buf, send, recv, r, j):
        at = (back - r) * size + j
        return remote(
            buf.at[at], buf.at[at - size], send.at[r, j], recv.at[r, j], pos + size
        )

    def send_up(buf, send, recv, r, j):
        pl.when(jnp.logical_and(has_up, pos >= r * size))(
            lambda: up(buf, send, recv, r, j).start()
        )

    def arrived(buf, send, recv, r, j):
        pl.when(pos >= r * size)(lambda: up(buf, send, recv, r - 1, j).wait_recv())

    for r in range(1, back + 1):
        def clear(r=r):
            for j in range(size):
                kbuf[(back - r) * size + j] = jnp.zeros(kbuf.shape[1:], BF16)
                vbuf[(back - r) * size + j] = jnp.zeros(vbuf.shape[1:], BF16)
        pl.when(pos < r * size)(clear)

    def clear_state():
        s_in[...] = jnp.zeros(s_in.shape, F32)
    pl.when(jnp.logical_not(has_down))(clear_state)

    first = unroll // mine
    for step in range(1, first):
        for which in (5, 0, 1, 2):
            deal(which, step).wait_recv()
    for which in (3, 4):
        for step in range(1, size):
            deal(which, step).start()

    rows = lax.broadcasted_iota(jnp.int32, (tok, tok), 0)
    cols = lax.broadcasted_iota(jnp.int32, (tok, tok), 1)
    levels = tok.bit_length() - 1

    def prep(index, carry):
        apart = jnp.bitwise_xor(rows, cols)
        diagonal = (rows == cols).astype(F32)
        lane = lax.broadcasted_iota(jnp.int32, rate_ref.shape, 1)
        members = range(unroll)
        turn_of = [index * unroll + i for i in members]
        head_of = [lax.rem(u, mine) for u in turn_of]
        block_of = [lax.rem(place - u // mine + size, size) for u in turn_of]
        unit_of = [block_of[i] * mine + head_of[i] for i in members]
        q_unit = [unit_rows(parts[1, block_of[i], :, columns_of(head_of[i])]) for i in members]
        k_unit = [unit_rows(parts[0, block_of[i], :, columns_of(head_of[i])]) for i in members]
        rate = [
            jnp.sum(
                jnp.where(lane == place * mine + head_of[i], rates[block_of[i]], 0.0),
                axis=1, keepdims=True,
            )
            for i in members
        ]
        k_split = [split(k) for k in k_unit]
        below = [
            jnp.where(rows > cols, rate[i] * dot3(k_split[i], k_split[i], NT), 0.0) for i in members
        ]
        inverse = [diagonal - jnp.where(apart == 1, below[i], 0.0) for i in members]
        for level in range(1, levels):
            now = (apart >> level) == 1
            part = [jnp.where(now, below[i], 0.0).astype(BF16) for i in members]
            short = [inverse[i].astype(BF16) for i in members]
            inner = [dot1(part[i], short[i]).astype(BF16) for i in members]
            inverse = [inverse[i] - dot1(short[i], inner[i]) for i in members]
        rest = [
            (inverse[i] - diagonal) + dot3(split(below[i]), split(inverse[i])) for i in members
        ]
        inverse = [
            inverse[i] - dot1(inverse[i].astype(BF16), rest[i].astype(BF16)) for i in members
        ]
        targets = [
            jnp.concatenate(
                [rate[i] * k_unit[i], rate[i] * parts[2, block_of[i], :, columns_of(head_of[i])].astype(F32)], axis=1
            )
            for i in members
        ]
        solved = [split(dot3(split(inverse[i]), split(targets[i]))) for i in members]
        for i in members:
            h = unit_of[i]
            cross = jnp.where(rows >= cols, dot3(split(q_unit[i]), k_split[i], NT), 0.0)
            mixed = dot3(split(cross), solved[i])
            l_buf[h] = q_unit[i] - mixed[:, :HEAD]
            b_buf[h] = mixed[:, HEAD:]
            moved = dot3(split(k_unit[i].T), solved[i])
            m_buf[h] = diagonal[:HEAD, :HEAD] - moved[:, :HEAD]
            c_buf[h] = moved[:, HEAD:]

        def keys_on():
            for step in range(first, size):
                for which in (5, 0, 1, 2):
                    deal(which, step).wait_recv()
            for step in range(1, size):
                deal(3, step).wait_recv()
            for j in range(size):
                send_up(kbuf, k_send, k_recv, 0, j)
        pl.when(index == 0)(keys_on)
        return carry

    lax.fori_loop(0, units // unroll, prep, 0)

    for step in range(1, size):
        deal(4, step).wait_recv()

    def weigh(h, carry):
        scale = 1.0 / math.sqrt(HEAD)
        h = units - 1 - h
        block = h // mine
        at = columns_of(lax.rem(h, mine))
        query = parts[4, block, :, at]
        top = None
        for slot in range(reach + 1):
            keys = kbuf[reach + block - slot, :, at]
            now = dot1(query, keys, NT) * scale
            if slot == 0:
                now = jnp.where(cols <= rows, now, -1e30)
            elif slot == reach:
                now = jnp.where(jnp.logical_and(cols > rows, base + block >= slot), now, -1e30)
            else:
                now = jnp.where(base + block >= slot, now, -1e30)
            scores[slot] = now
            top = now if top is None else jnp.maximum(top, now)
        top = jnp.max(top, axis=1, keepdims=True)
        total = jnp.zeros((tok, tok), F32)
        for slot in range(reach + 1):
            now = jnp.exp(scores[slot] - top)
            scores[slot] = now
            total = total + now
        scale_rows = 1.0 / jnp.sum(total, axis=1, keepdims=True)
        for slot in range(reach + 1):
            wbuf[h, slot] = (scores[slot] * scale_rows).astype(BF16)
        return carry

    def state_copy(i):
        return remote(s_out.at[i], s_in.at[i], s_send.at[i], s_recv.at[i], pos + size)

    whole = [jnp.concatenate([m_buf[i], c_buf[i]], axis=1) for i in range(mine)]
    for j in range(1, size):
        for i in range(mine):
            u = j * mine + i
            moved = dot3(split(m_buf[u]), split(whole[i]))
            whole[i] = jnp.concatenate([moved[:, :HEAD], moved[:, HEAD:] + c_buf[u]], axis=1)
    for i in range(mine):
        t_buf[i] = whole[i]

    for r in range(1, back):
        for j in range(size):
            arrived(kbuf, k_send, k_recv, r, j)
            send_up(kbuf, k_send, k_recv, r, j)

    last = jnp.logical_and(has_down, jnp.logical_not(has_up))
    some = jnp.where(pos >= reach, units // 4, 0)
    early = jnp.where(last, units, some)

    def far_keys():
        for j in range(size):
            arrived(kbuf, k_send, k_recv, back, j)

    pl.when(early > 0)(far_keys)
    lax.fori_loop(0, early, weigh, 0)

    for i in range(mine):
        pl.when(has_down)(lambda: state_copy(i).wait_recv())
        s_out[i] = dot3(split(t_buf[i, :, :HEAD]), split(s_in[i])) + t_buf[i, :, HEAD:]
        pl.when(has_up)(lambda: state_copy(i).start())
    state = [s_in[i] for i in range(mine)]
    for j in range(size):
        for i in range(mine):
            u = j * mine + i
            now = split(state[i])
            vbuf[reach + j, :, i * HEAD:(i + 1) * HEAD] = (
                dot3(split(l_buf[u]), now) + b_buf[u]
            ).astype(BF16)
            if j + 1 < size:
                state[i] = dot3(split(m_buf[u]), now) + c_buf[u]
        send_up(vbuf, v_send, v_recv, 0, j)

    def give_delta(step):
        to = peer(step)
        return remote(
            vbuf.at[reach + to], delta_ref.at[:, own_cols], d_send.at[step], d_recv.at[step],
            base + to,
        )

    for step in range(1, size):
        give_delta(step).start()
    delta_ref[:, own_cols] = vbuf[reach + place]

    pl.when(early == 0)(far_keys)
    half = early + (units - early) // 4
    lax.fori_loop(early, half, weigh, 0)
    for r in range(1, back):
        for j in range(size):
            arrived(vbuf, v_send, v_recv, r, j)
            send_up(vbuf, v_send, v_recv, r, j)
    lax.fori_loop(half, units, weigh, 0)
    for j in range(size):
        arrived(vbuf, v_send, v_recv, back, j)

    def give_att(step):
        to = peer(step)
        return remote(
            att.at[to], att_in.at[place], a_send.at[step], a_recv.at[step], base + to
        )

    def mix(step, carry):
        block = lax.rem(place + step, size)
        for i in range(mine):
            at = slice(i * HEAD, (i + 1) * HEAD)
            mixed = jnp.zeros((tok, HEAD), F32)
            for slot in range(reach + 1):
                mixed = mixed + dot1(
                    wbuf[block * mine + i, slot], vbuf[reach + block - slot, :, at]
                )
            att[block, :, at] = mixed.astype(BF16)
        return carry

    for step in range(1, size):
        mix(step, 0)
        give_att(step).start()
    mix(0, 0)
    att_in[place] = att[place]
    for step in range(1, size):
        give_att(step).wait_recv()

    squares = jnp.zeros((tok, wide), F32)
    for j in range(size):
        now = att_in[j].astype(F32)
        squares = squares + now * now
    sq_out[...] = jnp.broadcast_to(jnp.sum(squares, axis=1, keepdims=True), (tok, HEAD))
    total_sq = sq_out[...]
    trades = []
    for step in range(1, nh):
        trade = pltpu.make_async_remote_copy(
            src_ref=sq_out, dst_ref=sq_in.at[step - 1], send_sem=sq_send.at[step - 1],
            recv_sem=sq_recv.at[step - 1], device_id={"head": lax.rem(core + step, nh)},
            device_id_type=pl.DeviceIdType.MESH,
        )
        trade.start()
        trades.append(trade)
    for step, trade in enumerate(trades):
        trade.wait_recv()
        total_sq = total_sq + sq_in[step]
    scale_rows = lax.rsqrt(total_sq / (heads * HEAD * nh) + 1e-06)
    for j in range(size):
        for i in range(mine):
            at = slice((j * mine + i) * HEAD, (j * mine + i + 1) * HEAD)
            now = att_in[j, :, i * HEAD:(i + 1) * HEAD].astype(F32)
            norm_ref[:, at] = (now * gain_ref[:, at] * scale_rows).astype(BF16)

    for trade in trades:
        trade.wait_send()
    for step in range(1, size):
        give_delta(step).wait()
        give_att(step).wait_send()
        for which in range(6):
            deal(which, step).wait_send()

    def sent_up():
        for i in range(mine):
            state_copy(i).wait_send()
        for r in range(back):
            for j in range(size):
                pl.when(pos >= r * size)(lambda: up(kbuf, k_send, k_recv, r, j).wait_send())
                pl.when(pos >= r * size)(lambda: up(vbuf, v_send, v_recv, r, j).wait_send())
    pl.when(has_up)(sent_up)


def on_device(n, nh, q_delta, k_delta, v_delta, write_rate, q_attn, k_attn, out_gain):
    tok, features = q_delta.shape
    heads = write_rate.shape[1]
    size = PLANE
    while heads % size or n % size:
        size //= 2
    mine = heads // size
    wide = mine * HEAD
    unroll = 4 if heads % 4 == 0 else 1
    reach = WINDOW // tok
    back = reach // size
    assert reach % size == 0 and features == heads * HEAD
    vmem = pl.BlockSpec(memory_space=pltpu.VMEM)
    dma = pltpu.SemaphoreType.DMA
    return pl.pallas_call(
        functools.partial(kernel, n, nh, heads, size, reach, unroll, tok),
        out_shape=[jax.ShapeDtypeStruct((tok, features), BF16)] * 2,
        in_specs=[vmem] * 7,
        out_specs=[vmem] * 2,
        scratch_shapes=[
            pltpu.VMEM((5, size, tok, wide), BF16),
            pltpu.VMEM((size, tok, heads), F32),
            pltpu.VMEM((reach + size, tok, wide), BF16),
            pltpu.VMEM((reach + size, tok, wide), BF16),
            pltpu.VMEM((heads, reach + 1, tok, tok), BF16),
            pltpu.VMEM((reach + 1, tok, tok), F32),
            pltpu.VMEM((heads, HEAD, HEAD), F32),
            pltpu.VMEM((heads, HEAD, HEAD), F32),
            pltpu.VMEM((heads, tok, HEAD), F32),
            pltpu.VMEM((heads, tok, HEAD), F32),
            pltpu.VMEM((mine, HEAD, HEAD), F32),
            pltpu.VMEM((mine, HEAD, HEAD), F32),
            pltpu.VMEM((mine, HEAD, 2 * HEAD), F32),
            pltpu.VMEM((size, tok, wide), BF16),
            pltpu.VMEM((size, tok, wide), BF16),
            pltpu.VMEM((tok, HEAD), F32),
            pltpu.VMEM((max(nh - 1, 1), tok, HEAD), F32),
            dma((6, size)), dma((6, size)),
            dma((back, size)), dma((back, size)), dma((back, size)), dma((back, size)),
            dma((mine,)), dma((mine,)), dma((size,)), dma((size,)), dma((size,)), dma((size,)),
            dma((max(nh - 1, 1),)), dma((max(nh - 1, 1),)),
        ],
        compiler_params=pltpu.CompilerParams(
            collective_id=0, has_side_effects=True, vmem_limit_bytes=56 * 1024 * 1024
        ),
        cost_estimate=pl.CostEstimate(
            flops=10_000_000_000, bytes_accessed=8_000_000, transcendentals=5_000_000
        ),
    )(q_delta, k_delta, v_delta, write_rate, q_attn, k_attn, out_gain.reshape(1, features))


def solution(mesh):
    placed = (P("seq", "head"),) * 6 + (P("head"),)
    return jax.shard_map(
        functools.partial(on_device, mesh.shape["seq"], mesh.shape["head"]),
        mesh=mesh,
        in_specs=placed,
        out_specs=(P("seq", "head"), P("seq", "head")),
        check_vma=False,
    )
```
